32 devices in a mesh: row: 2 (over x), col: 16 (over z, y, core).
Axes of the slice: x: 2, y: 2, z: 4, core: 2. Of those that a mesh axis runs over, the one named last changes fastest.
Arguments:
- symmetric: float32 [12288, 12288], P('row', 'col'), may hold values from -24 to 24, as said below
Outputs:
- reduced: float32 [12288, 12288], P('row', 'col')
The draws below stay inside these ranges and needn't reach their ends.
Inputs may be any that keep to these rules, and one draw needn't show every extreme that they name: symmetric equals its transpose.
All inputs are finite; a program needn't handle non-finite values.
Results may differ from the reference program's by a relative error of at most 0.0001.
Values sent between devices are 32-bit elements; how exact they have to be, the bound alone decides.
A program may use at most 128 MiB of HBM per device.

```python
import math
import jax
import jax.numpy as jnp
from jax import lax

N = 12288
B = 256
PANELS = 1


def draw_symmetric(key, part):
    raw = jax.random.normal(jax.random.fold_in(key, 11), (N, N), jnp.float32)
    result = jnp.clip((raw + raw.T) * 0.70710678, -6.0, 6.0)
    return result


def setup_inputs(seed: int = 0) -> dict:
    keys = jax.random.split(jax.random.key(seed), 2)
    return {
        "symmetric": draw_symmetric(jax.random.fold_in(keys[1], 71), 0),
    }


HIGH = lax.Precision.HIGHEST

def matmul(left_op, right_op):
    return jnp.dot(left_op.astype(jnp.float32), right_op.astype(jnp.float32), precision=HIGH, preferred_element_type=jnp.float32)

def reference(symmetric):
    current = symmetric
    identity = jnp.eye(B, dtype=jnp.float32)
    positions = jnp.arange(N)
    factors = []
    for which in range(PANELS):
        first_col = which * B
        below = first_col + B
        panel_cols = jnp.where((positions >= below)[:, None], current[:, first_col:first_col + B], jnp.float32(0.0))
        gram = matmul(panel_cols.T, panel_cols)
        lower_factor = jnp.linalg.cholesky(gram)
        basis = lax.linalg.triangular_solve(lower_factor, panel_cols, left_side=False, lower=True, transpose_a=True)
        leading = basis[below:below + B]
        reflector = basis.at[below:below + B].add(-identity)
        t_mat = jnp.linalg.solve(identity - leading, identity)
        u_mat = matmul(current, reflector)
        core_sum = matmul(reflector.T, u_mat)
        middle = matmul(matmul(t_mat, core_sum), t_mat.T)
        w_mat = matmul(u_mat, t_mat.T) - 0.5 * matmul(reflector, middle)
        current = current - matmul(reflector, w_mat.T) - matmul(w_mat, reflector.T)
        factors.append(lower_factor.T)
    inverse_root = jnp.float32(1.0 / math.sqrt(N))
    for which in range(PANELS):
        first_col = which * B
        below = first_col + B
        block_vals = jnp.zeros((N - below, B), jnp.float32).at[:B].set(factors[which] * inverse_root)
        current = current.at[below:, first_col:first_col + B].set(block_vals)
        current = current.at[first_col:first_col + B, below:].set(block_vals.T)
    return current
```

```python
import math

import jax
import jax.numpy as jnp
from jax import lax
from jax.experimental import pallas as pl
from jax.experimental.pallas import tpu as pltpu
from jax.sharding import PartitionSpec as P

B = 256
NB = 64
TILE = 512
HIGH = lax.Precision.HIGH
HIGHEST = lax.Precision.HIGHEST
VMEM = pl.BlockSpec(memory_space=pltpu.VMEM)


def contract(left_op, right_op, left_dim, right_dim, precision=HIGHEST):
    return lax.dot_general(
        left_op,
        right_op,
        (((left_dim,), (right_dim,)), ((), ())),
        precision=precision,
        preferred_element_type=jnp.float32,
    )


def eye(n):
    rows = lax.broadcasted_iota(jnp.int32, (n, n), 0)
    cols = lax.broadcasted_iota(jnp.int32, (n, n), 1)
    return (rows == cols).astype(jnp.float32)


def eliminate(block, full):
    whole = jnp.concatenate([block, eye(NB)], axis=1)
    parts = [whole[8 * g : 8 * g + 8] for g in range(NB // 8)]
    sub = lax.broadcasted_iota(jnp.int32, (8, 2 * NB), 0)
    for j in range(NB):
        home, at = j // 8, j % 8
        row = parts[home][at : at + 1, :]
        scaled = row * (1.0 / row[:, j : j + 1])
        for g in range(0 if full else home, NB // 8):
            moved = parts[g] - parts[g][:, j : j + 1] * scaled
            if g == home:
                if full:
                    moved = jnp.where(sub == at, scaled, moved)
                else:
                    moved = jnp.where(sub > at, moved, parts[g])
            parts[g] = moved
    return jnp.concatenate(parts, axis=0)


def factor_kernel(gram_ref, r_ref, linv_ref, work):
    work[:, :B] = gram_ref[...]
    work[:, B:] = eye(B)
    for o in range(0, B, NB):
        done = eliminate(work[o : o + NB, o : o + NB], False)
        diag = jnp.sum(done[:, :NB] * eye(NB), axis=1, keepdims=True)
        scaled = done[:, NB:] * lax.rsqrt(diag)
        strip = contract(scaled, work[o : o + NB, :], 1, 0)
        rows = o + lax.broadcasted_iota(jnp.int32, (NB, B), 0)
        cols = lax.broadcasted_iota(jnp.int32, (NB, B), 1)
        r_ref[o : o + NB, :] = jnp.where(cols >= rows, strip[:, :B], 0.0)
        linv_ref[o : o + NB, :] = strip[:, B:]
        if o + NB < B:
            below = contract(strip[:, :B], strip, 0, 0)
            work[o + NB :, :] = work[o + NB :, :] - below[o + NB :, :]


def factor(gram):
    out = jax.ShapeDtypeStruct((B, B), jnp.float32)
    return pl.pallas_call(
        factor_kernel,
        out_shape=(out, out),
        in_specs=[VMEM],
        out_specs=(VMEM, VMEM),
        scratch_shapes=[pltpu.VMEM((B, 2 * B), jnp.float32)],
    )(gram)


def inverse_kernel(lead_t_ref, linv_ref, t_ref, work):
    work[:, :B] = eye(B) - contract(lead_t_ref[...], linv_ref[...], 0, 1)
    work[:, B:] = eye(B)
    for o in range(0, B, NB):
        done = eliminate(work[o : o + NB, o : o + NB], True)
        strip = contract(done[:, NB:], work[o : o + NB, :], 1, 0)
        change = contract(work[:, o : o + NB], strip, 1, 0)
        work[...] = work[...] - change
        work[o : o + NB, :] = strip
    t_ref[...] = work[:, B:]


def inverse(lead_t, linv):
    return pl.pallas_call(
        inverse_kernel,
        out_shape=jax.ShapeDtypeStruct((B, B), jnp.float32),
        in_specs=[VMEM, VMEM],
        out_specs=VMEM,
        scratch_shapes=[pltpu.VMEM((B, 2 * B), jnp.float32)],
    )(lead_t, linv)


def split(value):
    high = value.astype(jnp.bfloat16)
    low = (value - high.astype(jnp.float32)).astype(jnp.bfloat16)
    return high, low


def update_kernel(scale, a_ref, p_ref, u_ref, x1_ref, y_ref, x_ref, r_ref, o_ref, right):
    step = pl.program_id(0)
    row_at = lax.axis_index("row")
    col_at = lax.axis_index("col")
    cols_dev = a_ref.shape[1]

    @pl.when(step == 0)
    def _():
        for at, ref in ((0, x1_ref), (3, y_ref)):
            high, low = split(ref[...])
            right[at * B : (at + 1) * B, :] = high
            right[(at + 1) * B : (at + 2) * B, :] = high
            right[(at + 2) * B : (at + 3) * B, :] = low

    p_high, p_low = split(p_ref[...])
    u_high, u_low = split(u_ref[...])
    left = jnp.concatenate([p_high, p_low, p_high, u_high, u_low, u_high], axis=1)
    o_ref[...] = a_ref[...] - jnp.dot(left, right[...], preferred_element_type=jnp.float32)

    first = jnp.logical_and(step == 0, row_at == 0)

    @pl.when(first)
    def _():
        o_ref[B : 2 * B, :] = o_ref[B : 2 * B, :] + x_ref[...]
        global_cols = col_at * cols_dev + lax.broadcasted_iota(jnp.int32, (B, cols_dev), 1)
        band = lax.broadcasted_iota(jnp.int32, (B, cols_dev), 0)
        onehot = (global_cols - B == band).astype(jnp.float32)
        mirror = contract(r_ref[...] * scale, onehot, 0, 0)
        o_ref[:B, :] = jnp.where(global_cols >= B, mirror, o_ref[:B, :])

    @pl.when(jnp.logical_and(first, col_at == 0))
    def _():
        o_ref[B : 2 * B, :B] = r_ref[...] * scale

    @pl.when(jnp.logical_and(jnp.logical_not(first), col_at == 0))
    def _():
        o_ref[:, :B] = jnp.zeros((TILE, B), jnp.float32)


def update(current, panel, u_rows, x1, y, x, r_mat, order):
    rows_dev, cols_dev = current.shape
    tall = pl.BlockSpec((TILE, B), lambda i: (i, 0))
    flat = pl.BlockSpec((B, cols_dev), lambda i: (0, 0))
    wide = pl.BlockSpec((TILE, cols_dev), lambda i: (i, 0))
    scale = 1.0 / math.sqrt(order)

    def kernel(*refs):
        update_kernel(scale, *refs)

    return pl.pallas_call(
        kernel,
        grid=(rows_dev // TILE,),
        out_shape=jax.ShapeDtypeStruct((rows_dev, cols_dev), jnp.float32),
        in_specs=[wide, tall, tall, flat, flat, flat, pl.BlockSpec((B, B), lambda i: (0, 0))],
        out_specs=wide,
        scratch_shapes=[pltpu.VMEM((6 * B, cols_dev), jnp.bfloat16)],
        compiler_params=pltpu.CompilerParams(vmem_limit_bytes=48 * 1024 * 1024),
    )(current, panel, u_rows, x1, y, x, r_mat)


def spread(chunk, n_row, n_col, same_plane):
    rows = chunk.shape[0] // n_row
    piece = None
    for h in range(n_row):
        pairs = []
        for g in range(h, n_row * n_col, n_row):
            plane = g // n_col if same_plane else 0
            pairs.append((plane * n_col + g // n_row, g))
        moved = lax.ppermute(chunk[h * rows : (h + 1) * rows], ("row", "col"), pairs)
        piece = moved if piece is None else piece + moved
    return lax.all_gather(piece, "col", axis=0, tiled=True)


def per_device(n_row, n_col, symmetric):
    rows_dev, cols_dev = symmetric.shape
    order = cols_dev * n_col
    row_at = lax.axis_index("row")
    col_at = lax.axis_index("col")
    global_cols = col_at * cols_dev + jnp.arange(cols_dev, dtype=jnp.int32)
    band_index = jnp.arange(B, dtype=jnp.int32)
    is_top = row_at == 0

    strip = jnp.where((global_cols >= B)[None, :], symmetric[:B], jnp.float32(0.0))
    col_unit = (band_index[:, None] == global_cols[None, :] - B).astype(jnp.float32)
    panel = spread(strip.T, n_row, n_col, False)

    own = jnp.where(is_top, strip, jnp.float32(0.0))
    gram_part = contract(own, own, 1, 1)
    lead_part = contract(own, col_unit, 1, 1)
    gram, lead_t = lax.psum((gram_part, lead_part), ("row", "col"))
    tops = jnp.concatenate([own, jnp.where(is_top, symmetric[B : 2 * B], 0.0)], axis=0)
    tops = lax.psum(tops, "row")
    p_col, e_col = tops[:B], tops[B:]

    r_mat, linv = factor(gram)
    t_mat = inverse(lead_t, linv)
    v_col = contract(linv, p_col, 1, 0) - col_unit

    q_col = lax.psum(contract(panel, symmetric, 0, 0, HIGH), "row")
    u_col = contract(linv, q_col, 1, 0) - e_col
    u_rows = spread(u_col.T, n_row, n_col, True)
    core_sum = lax.psum(contract(v_col, u_col, 1, 1), "col")
    middle = contract(contract(t_mat, core_sum, 1, 0), t_mat, 1, 1)
    x = contract(t_mat, u_col, 1, 0) - contract(middle, v_col, 1, 0)
    y = contract(t_mat, v_col, 0, 0)
    x1 = contract(linv, x, 0, 0)
    return update(symmetric, panel, u_rows, x1, y, x, r_mat, order)


def solution(mesh):
    n_row, n_col = mesh.shape["row"], mesh.shape["col"]

    def run(symmetric):
        return per_device(n_row, n_col, symmetric)

    return jax.shard_map(
        run, mesh=mesh, in_specs=(P("row", "col"),), out_specs=P("row", "col"), check_vma=False
    )
```

```python
import math

import jax
import jax.numpy as jnp
from jax import lax
from jax.experimental import pallas as pl
from jax.experimental.pallas import tpu as pltpu
from jax.sharding import PartitionSpec as P

B = 256
NB = 64
TILE = 512
SUB = 4
MESH = pl.DeviceIdType.MESH
HIGH = lax.Precision.HIGH
HIGHEST = lax.Precision.HIGHEST
VMEM = pl.BlockSpec(memory_space=pltpu.VMEM)


def contract(left_op, right_op, left_dim, right_dim, precision=HIGHEST):
    return lax.dot_general(
        left_op,
        right_op,
        (((left_dim,), (right_dim,)), ((), ())),
        precision=precision,
        preferred_element_type=jnp.float32,
    )


def eye(n):
    rows = lax.broadcasted_iota(jnp.int32, (n, n), 0)
    cols = lax.broadcasted_iota(jnp.int32, (n, n), 1)
    return (rows == cols).astype(jnp.float32)


def eliminate(block, full):
    whole = jnp.concatenate([block, eye(NB)], axis=1)
    parts = [whole[8 * g : 8 * g + 8] for g in range(NB // 8)]
    sub = lax.broadcasted_iota(jnp.int32, (8, 2 * NB), 0)
    for j in range(NB):
        home, at = j // 8, j % 8
        row = parts[home][at : at + 1, :]
        scaled = row * (1.0 / row[:, j : j + 1])
        for g in range(0 if full else home, NB // 8):
            moved = parts[g] - parts[g][:, j : j + 1] * scaled
            if g == home:
                if full:
                    moved = jnp.where(sub == at, scaled, moved)
                else:
                    moved = jnp.where(sub > at, moved, parts[g])
            parts[g] = moved
    return jnp.concatenate(parts, axis=0)


def factor_into(gram, r_ref, linv_ref, work):
    work[:, :B] = gram
    work[:, B:] = eye(B)
    for o in range(0, B, NB):
        done = eliminate(work[o : o + NB, o : o + NB], False)
        diag = jnp.sum(done[:, :NB] * eye(NB), axis=1, keepdims=True)
        scaled = done[:, NB:] * lax.rsqrt(diag)
        strip = contract(scaled, work[o : o + NB, :], 1, 0)
        rows = o + lax.broadcasted_iota(jnp.int32, (NB, B), 0)
        cols = lax.broadcasted_iota(jnp.int32, (NB, B), 1)
        r_ref[o : o + NB, :] = jnp.where(cols >= rows, strip[:, :B], 0.0)
        linv_ref[o : o + NB, :] = strip[:, B:]
        if o + NB < B:
            below = contract(strip[:, :B], strip, 0, 0)
            work[o + NB :, :] = work[o + NB :, :] - below[o + NB :, :]


def inverse_kernel(lead_ref, linv_ref, t_ref, work):
    work[:, :B] = eye(B) - contract(lead_ref[...], linv_ref[...], 1, 1)
    work[:, B:] = eye(B)
    for o in range(0, B, NB):
        done = eliminate(work[o : o + NB, o : o + NB], True)
        strip = contract(done[:, NB:], work[o : o + NB, :], 1, 0)
        change = contract(work[:, o : o + NB], strip, 1, 0)
        work[...] = work[...] - change
        work[o : o + NB, :] = strip
    t_ref[...] = work[:, B:]


def inverse(lead, linv):
    return pl.pallas_call(
        inverse_kernel,
        out_shape=jax.ShapeDtypeStruct((B, B), jnp.float32),
        in_specs=[VMEM, VMEM],
        out_specs=VMEM,
        scratch_shapes=[pltpu.VMEM((B, 2 * B), jnp.float32)],
    )(lead, linv)


def split(value):
    high = value.astype(jnp.bfloat16)
    low = (value - high.astype(jnp.float32)).astype(jnp.bfloat16)
    return high, low


def update_kernel(scale, a_ref, p_ref, u_ref, x1_ref, y_ref, x_ref, r_ref, o_ref, right):
    step = pl.program_id(0)
    row_at = lax.axis_index("row")
    col_at = lax.axis_index("col")
    cols_dev = a_ref.shape[1]

    @pl.when(step == 0)
    def _():
        for at, ref in ((0, x1_ref), (3, y_ref)):
            high, low = split(ref[...])
            right[at * B : (at + 1) * B, :] = high
            right[(at + 1) * B : (at + 2) * B, :] = high
            right[(at + 2) * B : (at + 3) * B, :] = low

    p_high, p_low = split(p_ref[...])
    u_high, u_low = split(u_ref[...])
    left = jnp.concatenate([p_high, p_low, p_high, u_high, u_low, u_high], axis=1)
    o_ref[...] = a_ref[...] - jnp.dot(left, right[...], preferred_element_type=jnp.float32)

    first = jnp.logical_and(step == 0, row_at == 0)

    @pl.when(first)
    def _():
        o_ref[B : 2 * B, :] = o_ref[B : 2 * B, :] + x_ref[...]
        global_cols = col_at * cols_dev + lax.broadcasted_iota(jnp.int32, (B, cols_dev), 1)
        band = lax.broadcasted_iota(jnp.int32, (B, cols_dev), 0)
        onehot = (global_cols - B == band).astype(jnp.float32)
        mirror = contract(r_ref[...] * scale, onehot, 0, 0)
        o_ref[:B, :] = jnp.where(global_cols >= B, mirror, o_ref[:B, :])

    @pl.when(jnp.logical_and(first, col_at == 0))
    def _():
        o_ref[B : 2 * B, :B] = r_ref[...] * scale

    @pl.when(jnp.logical_and(jnp.logical_not(first), col_at == 0))
    def _():
        o_ref[:, :B] = jnp.zeros((TILE, B), jnp.float32)


def update(current, panel, u_rows, x1, y, x, r_mat, order):
    rows_dev, cols_dev = current.shape
    tall = pl.BlockSpec((TILE, B), lambda i: (i, 0))
    flat = pl.BlockSpec((B, cols_dev), lambda i: (0, 0))
    wide = pl.BlockSpec((TILE, cols_dev), lambda i: (i, 0))
    scale = 1.0 / math.sqrt(order)

    def kernel(*refs):
        update_kernel(scale, *refs)

    return pl.pallas_call(
        kernel,
        grid=(rows_dev // TILE,),
        out_shape=jax.ShapeDtypeStruct((rows_dev, cols_dev), jnp.float32),
        in_specs=[wide, tall, tall, flat, flat, flat, pl.BlockSpec((B, B), lambda i: (0, 0))],
        out_specs=wide,
        scratch_shapes=[pltpu.VMEM((6 * B, cols_dev), jnp.bfloat16)],
        compiler_params=pltpu.CompilerParams(vmem_limit_bytes=48 * 1024 * 1024),
    )(current, panel, u_rows, x1, y, x, r_mat)


def ring_of(mesh):
    coords = [tuple(d.coords) for d in mesh.devices[0][::2]]
    moving = [i for i in range(3) if len({c[i] for c in coords}) > 1]
    index = {c: i for i, c in enumerate(coords)}
    long_axis, short_axis = moving[0], moving[-1]
    tall = sorted({c[long_axis] for c in coords})
    flat = sorted({c[short_axis] for c in coords})

    def chip(a, b):
        at = list(coords[0])
        at[long_axis], at[short_axis] = tall[a], flat[b]
        return index[tuple(at)]

    order = [chip(a, 0) for a in range(len(tall) - 1, -1, -1)]
    for a in range(len(tall)):
        across = range(1, len(flat)) if a % 2 == 0 else range(len(flat) - 1, 0, -1)
        order += [chip(a, b) for b in across]
    return order


def look_up(table, at):
    found = jnp.int32(table[0])
    for i in range(1, len(table)):
        found = jnp.where(at == i, jnp.int32(table[i]), found)
    return found


def gather_kernel(ring, n_row, hop, *refs):
    if hop:
        first_ref, extra_ref, out_ref, chunk_ref, beside_ref = refs[:5]
        own_sem, ring_send, ring_recv, sib_send, sib_recv, hop_send, hop_recv, beside_send, beside_recv = refs[5:]
    else:
        chunk_ref, out_ref, own_sem, ring_send, ring_recv, sib_send, sib_recv = refs
    row_at, col_at = lax.axis_index("row"), lax.axis_index("col")
    n = len(ring)
    rows = chunk_ref.shape[0]
    cut = rows // SUB
    chip, core = col_at // 2, lax.rem(col_at, 2)
    per_plane = n // n_row
    place = look_up([ring.index(i) for i in range(n)], chip)
    way = 1 - 2 * core
    next_col = 2 * look_up(ring, lax.rem(place + way + n, n)) + core
    prev_col = 2 * look_up(ring, lax.rem(place - way + n, n)) + core
    sib_col = 2 * chip + 1 - core

    barrier = pltpu.get_barrier_semaphore()
    for col in (next_col, prev_col, sib_col):
        pl.semaphore_signal(barrier, inc=1, device_id=(row_at, col), device_id_type=MESH)
    if hop:
        @pl.when(row_at == 0)
        def _():
            for other in range(1, n_row):
                pl.semaphore_signal(barrier, inc=1, device_id=(other, col_at), device_id_type=MESH)

        @pl.when(row_at > 0)
        def _():
            pl.semaphore_signal(barrier, inc=1, device_id=(0, col_at), device_id_type=MESH)
    greetings = 3 + (jnp.where(row_at == 0, n_row - 1, 1) if hop else 0)
    pl.semaphore_wait(barrier, greetings)

    def window(source, of_core, sub):
        start = (source * 2 + of_core) * rows + sub * cut
        return out_ref.at[pl.ds(pl.multiple_of(start, 8), cut)]

    def piece(sub):
        return chunk_ref.at[pl.ds(sub * cut, cut)]

    def hop_copy(other, sub):
        return pltpu.make_async_remote_copy(
            src_ref=first_ref.at[pl.ds(sub * cut, cut)],
            dst_ref=piece(sub),
            send_sem=hop_send.at[other - 1, sub],
            recv_sem=hop_recv.at[sub],
            device_id=(other, col_at),
            device_id_type=MESH,
        )

    def beside_copy(other):
        return pltpu.make_async_remote_copy(
            src_ref=extra_ref,
            dst_ref=beside_ref,
            send_sem=beside_send.at[other - 1],
            recv_sem=beside_recv,
            device_id=(other, col_at),
            device_id_type=MESH,
        )

    def ring_copy(source, sub, src):
        return pltpu.make_async_remote_copy(
            src_ref=src,
            dst_ref=window(source, core, sub),
            send_sem=ring_send.at[source, sub],
            recv_sem=ring_recv.at[source, sub],
            device_id=(row_at, next_col),
            device_id_type=MESH,
        )

    def sib_copy(source, of_core, sub, src):
        return pltpu.make_async_remote_copy(
            src_ref=src,
            dst_ref=window(source, of_core, sub),
            send_sem=sib_send.at[source, sub],
            recv_sem=sib_recv.at[source, sub],
            device_id=(row_at, sib_col),
            device_id_type=MESH,
        )

    def found(step):
        at = look_up(ring, lax.rem(place - way * step + n, n))
        source = at - row_at * per_plane
        valid = jnp.logical_and(source >= 0, source < per_plane)
        return valid, jnp.clip(source, 0, per_plane - 1)

    if hop:
        @pl.when(row_at == 0)
        def _():
            for sub in range(SUB):
                for other in range(1, n_row):
                    hop_copy(other, sub).start()
            for other in range(1, n_row):
                beside_copy(other).start()
            moves = [
                pltpu.make_async_copy(first_ref, chunk_ref, own_sem.at[0]),
                pltpu.make_async_copy(extra_ref, beside_ref, own_sem.at[1]),
            ]
            for move in moves:
                move.start()
            for move in moves:
                move.wait()

    valid_home, home = found(0)

    def own_copy(sub):
        return pltpu.make_async_copy(piece(sub), window(home, core, sub), own_sem.at[2 + sub])

    for sub in range(SUB):
        if hop:
            @pl.when(row_at > 0)
            def _():
                hop_copy(1, sub).wait_recv()

        @pl.when(valid_home)
        def _():
            ring_copy(home, sub, piece(sub)).start()
            sib_copy(home, core, sub, piece(sub)).start()
            own_copy(sub).start()

    def forward(step, carry):
        valid, source = found(step)

        @pl.when(valid)
        def _():
            for sub in range(SUB):
                src = window(source, core, sub)
                ring_copy(source, sub, src).wait_recv()

                @pl.when(step < n - 1)
                def _():
                    ring_copy(source, sub, src).start()

                sib_copy(source, core, sub, src).start()

        return carry

    lax.fori_loop(1, n, forward, 0)

    def finish(step, carry):
        valid, source = found(step)

        @pl.when(valid)
        def _():
            for sub in range(SUB):
                src = window(source, core, sub)
                sib_copy(source, 1 - core, sub, src).wait_recv()

                @pl.when(step < n - 1)
                def _():
                    ring_copy(source, sub, src).wait_send()

                sib_copy(source, core, sub, src).wait_send()

        return carry

    lax.fori_loop(0, n, finish, 0)

    @pl.when(valid_home)
    def _():
        for sub in range(SUB):
            own_copy(sub).wait()

    if hop:
        @pl.when(row_at == 0)
        def _():
            for other in range(1, n_row):
                for sub in range(SUB):
                    hop_copy(other, sub).wait_send()
                beside_copy(other).wait_send()

        @pl.when(row_at > 0)
        def _():
            beside_copy(1).wait_recv()


def gather(chunks, ring, n_row, hop):
    per_plane = len(ring) // n_row
    dma = pltpu.SemaphoreType.DMA
    rows = chunks[0].shape[0]

    def kernel(*refs):
        gather_kernel(ring, n_row, hop, *refs)

    whole = jax.ShapeDtypeStruct((rows * per_plane * 2, B), jnp.float32)
    part = jax.ShapeDtypeStruct((rows, B), jnp.float32)
    hops = [dma((n_row - 1, SUB)), dma((SUB,)), dma((n_row - 1,)), dma]
    anywhere = pl.BlockSpec(memory_space=pl.ANY)
    return pl.pallas_call(
        kernel,
        out_shape=(whole, part, part) if hop else whole,
        in_specs=[anywhere] * len(chunks),
        out_specs=(anywhere,) * 3 if hop else anywhere,
        scratch_shapes=[dma((2 + SUB,))] + [dma((per_plane, SUB))] * 4 + (hops if hop else []),
        compiler_params=pltpu.CompilerParams(collective_id=int(hop), has_side_effects=True),
    )(*chunks)


def peers(n_row, row_at):
    return [lax.rem(row_at + d, n_row) for d in range(1, n_row)]


def greet(n_row, row_at, col_at):
    barrier = pltpu.get_barrier_semaphore()
    for other in peers(n_row, row_at):
        pl.semaphore_signal(barrier, inc=1, device_id=(other, col_at), device_id_type=MESH)
    pl.semaphore_wait(barrier, n_row - 1)


def exchange(n_row, row_at, col_at, src, landing, send, recv):
    copies = []
    for at, other in enumerate(peers(n_row, row_at)):
        copy = pltpu.make_async_remote_copy(
            src_ref=src,
            dst_ref=landing.at[at],
            send_sem=send.at[at],
            recv_sem=recv.at[at],
            device_id=(other, col_at),
            device_id_type=MESH,
        )
        copy.start()
        copies.append(copy)
    return copies


def total(n_row, src, landing, copies):
    for copy in copies:
        copy.wait_recv()
    found = src[...]
    for at in range(n_row - 1):
        found = found + landing[at]
    return found


def basis_kernel(
    n_row, gram_ref, k_ref, lead_ref, p_ref, e_ref, r_ref, linv_ref, lead_out, u_ref, v_ref,
    work, gram_in, k_in, gram_send, gram_recv, k_send, k_recv, lead_send, lead_recv,
):
    row_at, col_at = lax.axis_index("row"), lax.axis_index("col")
    greet(n_row, row_at, col_at)
    gram_copies = exchange(n_row, row_at, col_at, gram_ref, gram_in, gram_send, gram_recv)

    def lead_copy(other):
        return pltpu.make_async_remote_copy(
            src_ref=lead_ref,
            dst_ref=lead_out,
            send_sem=lead_send.at[other - 1],
            recv_sem=lead_recv,
            device_id=(other, col_at),
            device_id_type=MESH,
        )

    k_copies = exchange(n_row, row_at, col_at, k_ref, k_in, k_send, k_recv)

    @pl.when(row_at == 0)
    def _():
        for other in range(1, n_row):
            lead_copy(other).start()
        lead_out[...] = lead_ref[...]

    gram = total(n_row, gram_ref, gram_in, gram_copies)
    factor_into(gram, r_ref, linv_ref, work)
    linv = linv_ref[...]
    cols_dev = p_ref.shape[0]
    global_cols = col_at * cols_dev + lax.broadcasted_iota(jnp.int32, (cols_dev, B), 0)
    band = lax.broadcasted_iota(jnp.int32, (cols_dev, B), 1)
    col_unit = (global_cols - B == band).astype(jnp.float32)
    v_ref[...] = contract(p_ref[...], linv, 1, 1) - col_unit
    q_col = total(n_row, k_ref, k_in, k_copies)
    u_ref[...] = contract(q_col, linv, 0, 1) - e_ref[...]
    for copy in gram_copies + k_copies:
        copy.wait_send()

    @pl.when(row_at == 0)
    def _():
        for other in range(1, n_row):
            lead_copy(other).wait_send()

    @pl.when(row_at > 0)
    def _():
        lead_copy(1).wait_recv()


def basis(n_row, gram, k, lead, p_col, e_col):
    dma = pltpu.SemaphoreType.DMA
    small = jax.ShapeDtypeStruct((B, B), jnp.float32)
    part = jax.ShapeDtypeStruct(p_col.shape, jnp.float32)
    others = dma((n_row - 1,))

    def kernel(*refs):
        basis_kernel(n_row, *refs)

    return pl.pallas_call(
        kernel,
        out_shape=(small, small, small, part, part),
        in_specs=[VMEM] * 5,
        out_specs=(VMEM,) * 5,
        scratch_shapes=[
            pltpu.VMEM((B, 2 * B), jnp.float32),
            pltpu.VMEM((n_row - 1, B, B), jnp.float32),
            pltpu.VMEM((n_row - 1,) + k.shape, jnp.float32),
            others, others, others, others, others, dma,
        ],
        compiler_params=pltpu.CompilerParams(
            collective_id=2, has_side_effects=True, vmem_limit_bytes=48 * 1024 * 1024
        ),
    )(gram, k, lead, p_col, e_col)


def middle_kernel(
    n_row, z_ref, t_ref, linv_ref, u_ref, v_ref, x_ref, x1_ref, y_ref, z_in, z_send, z_recv
):
    row_at, col_at = lax.axis_index("row"), lax.axis_index("col")
    greet(n_row, row_at, col_at)
    copies = exchange(n_row, row_at, col_at, z_ref, z_in, z_send, z_recv)
    t_mat = t_ref[...]
    y_ref[...] = contract(t_mat, v_ref[...], 0, 1)
    x_ref[...] = contract(t_mat, u_ref[...], 1, 1)
    core_sum = total(n_row, z_ref, z_in, copies)
    middle = contract(contract(t_mat, core_sum, 1, 0), t_mat, 1, 1)
    x = x_ref[...] - contract(middle, v_ref[...], 1, 1)
    x_ref[...] = x
    x1_ref[...] = contract(linv_ref[...], x, 0, 0)
    for copy in copies:
        copy.wait_send()


def middle_terms(n_row, z, t_mat, linv, u_col, v_col):
    dma = pltpu.SemaphoreType.DMA
    flat = jax.ShapeDtypeStruct(u_col.shape[::-1], jnp.float32)

    def kernel(*refs):
        middle_kernel(n_row, *refs)

    return pl.pallas_call(
        kernel,
        out_shape=(flat,) * 3,
        in_specs=[VMEM] * 5,
        out_specs=(VMEM,) * 3,
        scratch_shapes=[
            pltpu.VMEM((n_row - 1, B, B), jnp.float32), dma((n_row - 1,)), dma((n_row - 1,))
        ],
        compiler_params=pltpu.CompilerParams(
            collective_id=3, has_side_effects=True, vmem_limit_bytes=48 * 1024 * 1024
        ),
    )(z, t_mat, linv, u_col, v_col)


def per_device(ring, n_row, symmetric):
    cols_dev = symmetric.shape[1]
    order = symmetric.shape[0] * n_row
    row_at, col_at = lax.axis_index("row"), lax.axis_index("col")
    global_cols = col_at * cols_dev + jnp.arange(cols_dev, dtype=jnp.int32)
    is_top = row_at == 0

    strip = jnp.where((global_cols >= B)[None, :], symmetric[:B], jnp.float32(0.0))
    panel, p_col, e_col = gather((strip.T, symmetric[B : 2 * B].T), ring, n_row, True)
    gram_part = contract(panel, panel, 0, 0)
    k_part = contract(panel, symmetric, 0, 0, HIGH)
    r_mat, linv, lead, u_col, v_col = basis(
        n_row, gram_part, k_part, panel[B : 2 * B], p_col, e_col
    )
    t_mat = inverse(lead, linv)
    u_rows = gather((u_col,), ring, n_row, False)
    z = contract(linv, contract(panel, u_rows, 0, 0), 1, 0)
    z = z - jnp.where(is_top, u_rows[B : 2 * B], jnp.float32(0.0))
    x, x1, y = middle_terms(n_row, z, t_mat, linv, u_col, v_col)
    return update(symmetric, panel, u_rows, x1, y, x, r_mat, order)


def solution(mesh):
    n_row = mesh.shape["row"]

    ring = ring_of(mesh)

    def run(symmetric):
        return per_device(ring, n_row, symmetric)

    return jax.shard_map(
        run, mesh=mesh, in_specs=(P("row", "col"),), out_specs=P("row", "col"), check_vma=False
    )
```

```python
import math

import jax
import jax.numpy as jnp
from jax import lax
from jax.experimental import pallas as pl
from jax.experimental.pallas import tpu as pltpu
from jax.sharding import PartitionSpec as P

B = 256
NB = 64
TILE = 512
SUB = 8
MESH = pl.DeviceIdType.MESH
HIGH = lax.Precision.HIGH
HIGHEST = lax.Precision.HIGHEST
VMEM = pl.BlockSpec(memory_space=pltpu.VMEM)


def contract(left_op, right_op, left_dim, right_dim, precision=HIGHEST):
    return lax.dot_general(
        left_op,
        right_op,
        (((left_dim,), (right_dim,)), ((), ())),
        precision=precision,
        preferred_element_type=jnp.float32,
    )


def eye(n):
    rows = lax.broadcasted_iota(jnp.int32, (n, n), 0)
    cols = lax.broadcasted_iota(jnp.int32, (n, n), 1)
    return (rows == cols).astype(jnp.float32)


def eliminate_some(whole, columns, full):
    parts = [whole[8 * g : 8 * g + 8] for g in range(NB // 8)]
    sub = lax.broadcasted_iota(jnp.int32, (8, 2 * NB), 0)
    for j in columns:
        home, at = j // 8, j % 8
        row = parts[home][at : at + 1, :]
        scaled = row * (1.0 / row[:, j : j + 1])
        for g in range(0 if full else home, NB // 8):
            moved = parts[g] - parts[g][:, j : j + 1] * scaled
            if g == home:
                if full:
                    moved = jnp.where(sub == at, scaled, moved)
                else:
                    moved = jnp.where(sub > at, moved, parts[g])
            parts[g] = moved
    return jnp.concatenate(parts, axis=0)


def factor_into(gram, r_ref, linv_ref, work):
    work[:, :B] = gram
    work[:, B:] = eye(B)
    for o in range(0, B, NB):
        whole = jnp.concatenate([work[o : o + NB, o : o + NB], eye(NB)], axis=1)
        done = eliminate_some(whole, range(NB), False)
        diag = jnp.sum(done[:, :NB] * eye(NB), axis=1, keepdims=True)
        scaled = done[:, NB:] * lax.rsqrt(diag)
        strip = contract(scaled, work[o : o + NB, :], 1, 0)
        rows = o + lax.broadcasted_iota(jnp.int32, (NB, B), 0)
        cols = lax.broadcasted_iota(jnp.int32, (NB, B), 1)
        r_ref[o : o + NB, :] = jnp.where(cols >= rows, strip[:, :B], 0.0)
        linv_ref[o : o + NB, :] = strip[:, B:]
        if o + NB < B:
            below = contract(strip[:, :B], strip, 0, 0)
            work[o + NB :, :] = work[o + NB :, :] - below[o + NB :, :]


def update_kernel(scale, a_ref, p_ref, u_ref, x1_ref, y_ref, x_ref, r_ref, o_ref, right):
    step = pl.program_id(0)
    row_at = lax.axis_index("row")
    col_at = lax.axis_index("col")
    cols_dev = a_ref.shape[1]

    @pl.when(step == 0)
    def _():
        for at, ref in ((0, x1_ref), (3, y_ref)):
            high, low = split(ref[...])
            right[at * B : (at + 1) * B, :] = high
            right[(at + 1) * B : (at + 2) * B, :] = high
            right[(at + 2) * B : (at + 3) * B, :] = low

    p_high, p_low = split(p_ref[...])
    u_high, u_low = split(u_ref[...])
    left = jnp.concatenate([p_high, p_low, p_high, u_high, u_low, u_high], axis=1)
    o_ref[...] = a_ref[...] - jnp.dot(left, right[...], preferred_element_type=jnp.float32)

    first = jnp.logical_and(step == 0, row_at == 0)

    @pl.when(first)
    def _():
        o_ref[B : 2 * B, :] = o_ref[B : 2 * B, :] + x_ref[...]
        global_cols = col_at * cols_dev + lax.broadcasted_iota(jnp.int32, (B, cols_dev), 1)
        band = lax.broadcasted_iota(jnp.int32, (B, cols_dev), 0)
        onehot = (global_cols - B == band).astype(jnp.float32)
        mirror = contract(r_ref[...] * scale, onehot, 0, 0)
        o_ref[:B, :] = jnp.where(global_cols >= B, mirror, o_ref[:B, :])

    @pl.when(jnp.logical_and(first, col_at == 0))
    def _():
        o_ref[B : 2 * B, :B] = r_ref[...] * scale

    @pl.when(jnp.logical_and(jnp.logical_not(first), col_at == 0))
    def _():
        o_ref[:, :B] = jnp.zeros((TILE, B), jnp.float32)


def update(current, panel, u_rows, x1, y, x, r_mat, order):
    rows_dev, cols_dev = current.shape
    tall = pl.BlockSpec((TILE, B), lambda i: (i, 0))
    flat = pl.BlockSpec((B, cols_dev), lambda i: (0, 0))
    wide = pl.BlockSpec((TILE, cols_dev), lambda i: (i, 0))
    scale = 1.0 / math.sqrt(order)

    def kernel(*refs):
        update_kernel(scale, *refs)

    return pl.pallas_call(
        kernel,
        grid=(rows_dev // TILE,),
        out_shape=jax.ShapeDtypeStruct((rows_dev, cols_dev), jnp.float32),
        in_specs=[wide, tall, tall, flat, flat, flat, pl.BlockSpec((B, B), lambda i: (0, 0))],
        out_specs=wide,
        scratch_shapes=[pltpu.VMEM((6 * B, cols_dev), jnp.bfloat16)],
        compiler_params=pltpu.CompilerParams(vmem_limit_bytes=48 * 1024 * 1024),
    )(current, panel, u_rows, x1, y, x, r_mat)


def ring_of(mesh):
    coords = [tuple(d.coords) for d in mesh.devices[0][::2]]
    moving = [i for i in range(3) if len({c[i] for c in coords}) > 1]
    index = {c: i for i, c in enumerate(coords)}
    long_axis, short_axis = moving[0], moving[-1]
    tall = sorted({c[long_axis] for c in coords})
    flat = sorted({c[short_axis] for c in coords})

    def chip(a, b):
        at = list(coords[0])
        at[long_axis], at[short_axis] = tall[a], flat[b]
        return index[tuple(at)]

    order = [chip(a, 0) for a in range(len(tall) - 1, -1, -1)]
    for a in range(len(tall)):
        across = range(1, len(flat)) if a % 2 == 0 else range(len(flat) - 1, 0, -1)
        order += [chip(a, b) for b in across]
    return order


def look_up(table, at):
    found = jnp.int32(table[0])
    for i in range(1, len(table)):
        found = jnp.where(at == i, jnp.int32(table[i]), found)
    return found


def ring_gather(ring, n_row, out_ref, first_ref, sems):
    ring_send, ring_recv, sib_send, sib_recv = sems
    row_at, col_at = lax.axis_index("row"), lax.axis_index("col")
    n = len(ring)
    rows = first_ref.shape[0]
    cut = rows // SUB
    chip, core = col_at // 2, lax.rem(col_at, 2)
    per_plane = n // n_row
    place = look_up([ring.index(i) for i in range(n)], chip)
    way = 1 - 2 * core
    next_col = 2 * look_up(ring, lax.rem(place + way + n, n)) + core
    prev_col = 2 * look_up(ring, lax.rem(place - way + n, n)) + core
    sib_col = 2 * chip + 1 - core

    barrier = pltpu.get_barrier_semaphore()
    for col in (next_col, prev_col, sib_col):
        pl.semaphore_signal(barrier, inc=1, device_id=(row_at, col), device_id_type=MESH)
    for other in peers(n_row, row_at):
        pl.semaphore_signal(barrier, inc=1, device_id=(other, col_at), device_id_type=MESH)
    pl.semaphore_wait(barrier, 3 + n_row - 1)

    def start_of(source, of_core):
        return pl.multiple_of((source * 2 + of_core) * rows, 8)

    def window(source, of_core, sub):
        return out_ref.at[pl.ds(pl.multiple_of(start_of(source, of_core) + sub * cut, 8), cut)]

    def ring_copy(source, sub, src):
        return pltpu.make_async_remote_copy(
            src_ref=src,
            dst_ref=window(source, core, sub),
            send_sem=ring_send.at[source, sub],
            recv_sem=ring_recv.at[source, sub],
            device_id=(row_at, next_col),
            device_id_type=MESH,
        )

    def sib_copy(source, of_core, sub, src):
        return pltpu.make_async_remote_copy(
            src_ref=src,
            dst_ref=window(source, of_core, sub),
            send_sem=sib_send.at[source, sub],
            recv_sem=sib_recv.at[source, sub],
            device_id=(row_at, sib_col),
            device_id_type=MESH,
        )

    def found(step, turn):
        at = look_up(ring, lax.rem(place - turn * step + n, n))
        source = at - row_at * per_plane
        valid = jnp.logical_and(source >= 0, source < per_plane)
        return valid, jnp.clip(source, 0, per_plane - 1)

    has_home, home = found(0, way)

    def begin(sub, src_ref):
        src = src_ref.at[pl.ds(sub * cut, cut)]
        ring_copy(home, sub, src).start()
        sib_copy(home, core, sub, src).start()

    def keep(src_ref):
        out_ref[pl.ds(start_of(home, core), rows), :] = src_ref[...]

    def forward(step, sub):
        valid, source = found(step, way)

        @pl.when(valid)
        def _():
            src = window(source, core, sub)
            ring_copy(source, sub, src).wait_recv()

            @pl.when(step < n - 1)
            def _():
                ring_copy(source, sub, src).start()

            sib_copy(source, core, sub, src).start()

    def from_sibling(source):
        for sub in range(SUB):
            sib_copy(source, 1 - core, sub, window(source, core, sub)).wait_recv()

    def finish():
        def sent(step, carry):
            valid, source = found(step, way)

            @pl.when(valid)
            def _():
                for sub in range(SUB):
                    src = window(source, core, sub)

                    @pl.when(step < n - 1)
                    def _():
                        ring_copy(source, sub, src).wait_send()

                    sib_copy(source, core, sub, src).wait_send()

            return carry

        lax.fori_loop(0, n, sent, 0)

    return dict(
        n=n, way=way, core=core, has_home=has_home, start_of=start_of, found=found, begin=begin, keep=keep,
        forward=forward, from_sibling=from_sibling, finish=finish,
    )


def split(value):
    high = value.astype(jnp.bfloat16)
    low = (value - high.astype(jnp.float32)).astype(jnp.bfloat16)
    return high, low


def product(left_op, right_op):
    left_high, left_low = split(left_op)
    right_high, right_low = split(right_op)
    left = jnp.concatenate([left_high, left_low, left_high], axis=0)
    right = jnp.concatenate([right_high, right_high, right_low], axis=0)
    return lax.dot_general(
        left, right, (((0,), (0,)), ((), ())), preferred_element_type=jnp.float32
    )


def panel_kernel(
    ring, n_row, first_ref, extra_ref, a_ref, out_ref, chunk_ref, beside_ref, k_ref, gram_ref,
    held, a_sem, ring_send, ring_recv, sib_send, sib_recv, hop_send, hop_recv, beside_send, beside_recv,
):
    row_at, col_at = lax.axis_index("row"), lax.axis_index("col")
    rows = first_ref.shape[0]
    cut = rows // SUB
    load = pltpu.make_async_copy(a_ref, held, a_sem)
    load.start()
    g = ring_gather(ring, n_row, out_ref, first_ref, (ring_send, ring_recv, sib_send, sib_recv))
    has_home = g["has_home"]

    def hop_copy(other, sub):
        return pltpu.make_async_remote_copy(
            src_ref=first_ref.at[pl.ds(sub * cut, cut)],
            dst_ref=chunk_ref.at[pl.ds(sub * cut, cut)],
            send_sem=hop_send.at[other - 1, sub],
            recv_sem=hop_recv.at[sub],
            device_id=(other, col_at),
            device_id_type=MESH,
        )

    def beside_copy(other):
        return pltpu.make_async_remote_copy(
            src_ref=extra_ref,
            dst_ref=beside_ref,
            send_sem=beside_send.at[other - 1],
            recv_sem=beside_recv,
            device_id=(other, col_at),
            device_id_type=MESH,
        )

    @pl.when(row_at == 0)
    def _():
        for sub in range(SUB):
            @pl.when(has_home)
            def _():
                g["begin"](sub, first_ref)

            for other in range(1, n_row):
                hop_copy(other, sub).start()
        for other in range(1, n_row):
            beside_copy(other).start()
        chunk_ref[...] = first_ref[...]
        beside_ref[...] = extra_ref[...]

        @pl.when(has_home)
        def _():
            g["keep"](first_ref)

    @pl.when(jnp.logical_and(row_at > 0, has_home))
    def _():
        for sub in range(SUB):
            hop_copy(1, sub).wait_recv()
            g["begin"](sub, chunk_ref)
        g["keep"](chunk_ref)

    k_ref[...] = jnp.zeros_like(k_ref)
    gram_ref[...] = jnp.zeros_like(gram_ref)
    load.wait()

    def absorb(source, of_core):
        at = pl.ds(g["start_of"](source, of_core), rows)
        panel = out_ref[at, :]
        k_ref[...] += product(panel, held[at, :])
        gram_ref[...] += contract(panel, panel, 0, 0)

    def step_on(step, carry):
        valid, source = g["found"](step, g["way"])

        @pl.when(step > 0)
        def _():
            for sub in range(SUB):
                g["forward"](step, sub)

        @pl.when(valid)
        def _():
            absorb(source, g["core"])

        sib_valid, sib_source = g["found"](step, -g["way"])

        @pl.when(sib_valid)
        def _():
            g["from_sibling"](sib_source)
            absorb(sib_source, 1 - g["core"])

        return carry

    lax.fori_loop(0, g["n"], step_on, 0)
    g["finish"]()

    @pl.when(row_at == 0)
    def _():
        for other in range(1, n_row):
            for sub in range(SUB):
                hop_copy(other, sub).wait_send()
            beside_copy(other).wait_send()

    @pl.when(row_at > 0)
    def _():
        beside_copy(1).wait_recv()

    @pl.when(jnp.logical_and(row_at > 0, jnp.logical_not(has_home)))
    def _():
        for sub in range(SUB):
            hop_copy(1, sub).wait_recv()


def panel_terms(first, extra, symmetric, ring, n_row):
    per_plane = len(ring) // n_row
    dma = pltpu.SemaphoreType.DMA
    rows = first.shape[0]

    def kernel(*refs):
        panel_kernel(ring, n_row, *refs)

    def shape(*dims):
        return jax.ShapeDtypeStruct(dims, jnp.float32)

    return pl.pallas_call(
        kernel,
        out_shape=(
            shape(symmetric.shape[0], B), shape(rows, B), shape(rows, B), shape(B, rows), shape(B, B)
        ),
        in_specs=[VMEM, VMEM, pl.BlockSpec(memory_space=pl.ANY)],
        out_specs=(VMEM,) * 5,
        scratch_shapes=[pltpu.VMEM(symmetric.shape, jnp.float32), dma]
        + [dma((per_plane, SUB))] * 4
        + [dma((n_row - 1, SUB)), dma((SUB,)), dma((n_row - 1,)), dma],
        compiler_params=pltpu.CompilerParams(
            collective_id=1, has_side_effects=True, vmem_limit_bytes=56 * 1024 * 1024
        ),
    )(first, extra, symmetric)


def inverse_tasks(lead_ref, linv_ref, t_ref, work, block):
    tasks = []

    def begin():
        work[:, :B] = eye(B) - contract(lead_ref[...], linv_ref[...], 1, 1)
        work[:, B:] = eye(B)

    tasks.append(begin)
    for o in range(0, B, NB):
        def load(o=o):
            block[...] = jnp.concatenate([work[o : o + NB, o : o + NB], eye(NB)], axis=1)

        tasks.append(load)
        for j in range(0, NB, 4):
            def some(j=j):
                block[...] = eliminate_some(block[...], range(j, j + 4), True)

            tasks.append(some)

        def spread(o=o):
            strip = contract(block[:, NB:], work[o : o + NB, :], 1, 0)
            change = contract(work[:, o : o + NB], strip, 1, 0)
            work[...] = work[...] - change
            work[o : o + NB, :] = strip

        tasks.append(spread)

    def end():
        t_ref[...] = work[:, B:]

    tasks.append(end)
    return tasks


def product_kernel(
    ring, n_row, u_ref, v_ref, lead_ref, linv_ref, panel_ref, out_ref, x_ref, x1_ref, y_ref,
    t_ref, work, block, z_ref, z_in, ring_send, ring_recv, sib_send, sib_recv, z_send, z_recv,
):
    row_at, col_at = lax.axis_index("row"), lax.axis_index("col")
    rows = u_ref.shape[0]
    g = ring_gather(ring, n_row, out_ref, u_ref, (ring_send, ring_recv, sib_send, sib_recv))
    has_home, n = g["has_home"], g["n"]

    @pl.when(has_home)
    def _():
        for sub in range(SUB):
            g["begin"](sub, u_ref)
        g["keep"](u_ref)

    tasks = inverse_tasks(lead_ref, linv_ref, t_ref, work, block)
    slots = (n - 1) * SUB
    done = 0
    for slot in range(slots):
        g["forward"](1 + slot // SUB, slot % SUB)
        until = (slot + 1) * len(tasks) // slots
        for task in tasks[done:until]:
            task()
        done = until
    t_mat = t_ref[...]
    y_ref[...] = contract(t_mat, v_ref[...], 0, 1)
    x_ref[...] = contract(t_mat, u_ref[...], 1, 1)
    z_ref[...] = jnp.zeros_like(z_ref)

    def absorb(source, carry):
        g["from_sibling"](source)
        at = pl.ds(pl.multiple_of(source * 2 * rows, 8), 2 * rows)
        z_ref[...] += product(panel_ref[at, :], out_ref[at, :])
        return carry

    lax.fori_loop(0, n // n_row, absorb, 0)
    own = jnp.where(row_at == 0, out_ref[B : 2 * B, :], 0.0)
    z_ref[...] = contract(linv_ref[...], z_ref[...], 1, 0) - own
    copies = exchange(n_row, row_at, col_at, z_ref, z_in, z_send, z_recv)
    g["finish"]()
    core_sum = total(n_row, z_ref, z_in, copies)
    middle = contract(contract(t_mat, core_sum, 1, 0), t_mat, 1, 1)
    x = x_ref[...] - contract(middle, v_ref[...], 1, 1)
    x_ref[...] = x
    x1_ref[...] = contract(linv_ref[...], x, 0, 0)
    for copy in copies:
        copy.wait_send()


def product_terms(u_col, v_col, lead, linv, panel, ring, n_row):
    per_plane = len(ring) // n_row
    dma = pltpu.SemaphoreType.DMA
    flat = jax.ShapeDtypeStruct(u_col.shape[::-1], jnp.float32)

    def kernel(*refs):
        product_kernel(ring, n_row, *refs)

    def scratch(*dims):
        return pltpu.VMEM(dims, jnp.float32)

    return pl.pallas_call(
        kernel,
        out_shape=(jax.ShapeDtypeStruct(panel.shape, jnp.float32), flat, flat, flat),
        in_specs=[VMEM] * 5,
        out_specs=(VMEM,) * 4,
        scratch_shapes=[
            scratch(B, B), scratch(B, 2 * B), scratch(NB, 2 * NB), scratch(B, B), scratch(n_row - 1, B, B)
        ]
        + [dma((per_plane, SUB))] * 4
        + [dma((n_row - 1,))] * 2,
        compiler_params=pltpu.CompilerParams(
            collective_id=3, has_side_effects=True, vmem_limit_bytes=56 * 1024 * 1024
        ),
    )(u_col, v_col, lead, linv, panel)


def peers(n_row, row_at):
    return [lax.rem(row_at + d, n_row) for d in range(1, n_row)]


def greet(n_row, row_at, col_at):
    barrier = pltpu.get_barrier_semaphore()
    for other in peers(n_row, row_at):
        pl.semaphore_signal(barrier, inc=1, device_id=(other, col_at), device_id_type=MESH)
    pl.semaphore_wait(barrier, n_row - 1)


def exchange(n_row, row_at, col_at, src, landing, send, recv):
    copies = []
    for at, other in enumerate(peers(n_row, row_at)):
        copy = pltpu.make_async_remote_copy(
            src_ref=src,
            dst_ref=landing.at[at],
            send_sem=send.at[at],
            recv_sem=recv.at[at],
            device_id=(other, col_at),
            device_id_type=MESH,
        )
        copy.start()
        copies.append(copy)
    return copies


def total(n_row, src, landing, copies):
    for copy in copies:
        copy.wait_recv()
    found = src[...]
    for at in range(n_row - 1):
        found = found + landing[at]
    return found


def basis_kernel(
    n_row, gram_ref, k_ref, lead_ref, p_ref, e_ref, r_ref, linv_ref, lead_out, u_ref, v_ref,
    work, gram_in, k_in, gram_send, gram_recv, k_send, k_recv, lead_send, lead_recv,
):
    row_at, col_at = lax.axis_index("row"), lax.axis_index("col")
    greet(n_row, row_at, col_at)
    gram_copies = exchange(n_row, row_at, col_at, gram_ref, gram_in, gram_send, gram_recv)

    def lead_copy(other):
        return pltpu.make_async_remote_copy(
            src_ref=lead_ref,
            dst_ref=lead_out,
            send_sem=lead_send.at[other - 1],
            recv_sem=lead_recv,
            device_id=(other, col_at),
            device_id_type=MESH,
        )

    k_copies = exchange(n_row, row_at, col_at, k_ref, k_in, k_send, k_recv)

    @pl.when(row_at == 0)
    def _():
        for other in range(1, n_row):
            lead_copy(other).start()
        lead_out[...] = lead_ref[...]

    gram = total(n_row, gram_ref, gram_in, gram_copies)
    factor_into(gram, r_ref, linv_ref, work)
    linv = linv_ref[...]
    cols_dev = p_ref.shape[0]
    global_cols = col_at * cols_dev + lax.broadcasted_iota(jnp.int32, (cols_dev, B), 0)
    band = lax.broadcasted_iota(jnp.int32, (cols_dev, B), 1)
    col_unit = (global_cols - B == band).astype(jnp.float32)
    v_ref[...] = contract(p_ref[...], linv, 1, 1) - col_unit
    q_col = total(n_row, k_ref, k_in, k_copies)
    u_ref[...] = contract(q_col, linv, 0, 1) - e_ref[...]
    for copy in gram_copies + k_copies:
        copy.wait_send()

    @pl.when(row_at == 0)
    def _():
        for other in range(1, n_row):
            lead_copy(other).wait_send()

    @pl.when(row_at > 0)
    def _():
        lead_copy(1).wait_recv()


def basis(n_row, gram, k, lead, p_col, e_col):
    dma = pltpu.SemaphoreType.DMA
    small = jax.ShapeDtypeStruct((B, B), jnp.float32)
    part = jax.ShapeDtypeStruct(p_col.shape, jnp.float32)
    others = dma((n_row - 1,))

    def kernel(*refs):
        basis_kernel(n_row, *refs)

    return pl.pallas_call(
        kernel,
        out_shape=(small, small, small, part, part),
        in_specs=[VMEM] * 5,
        out_specs=(VMEM,) * 5,
        scratch_shapes=[
            pltpu.VMEM((B, 2 * B), jnp.float32),
            pltpu.VMEM((n_row - 1, B, B), jnp.float32),
            pltpu.VMEM((n_row - 1,) + k.shape, jnp.float32),
            others, others, others, others, others, dma,
        ],
        compiler_params=pltpu.CompilerParams(
            collective_id=2, has_side_effects=True, vmem_limit_bytes=48 * 1024 * 1024
        ),
    )(gram, k, lead, p_col, e_col)


def per_device(ring, n_row, symmetric):
    cols_dev = symmetric.shape[1]
    order = symmetric.shape[0] * n_row
    global_cols = lax.axis_index("col") * cols_dev + jnp.arange(cols_dev, dtype=jnp.int32)

    strip = jnp.where((global_cols >= B)[None, :], symmetric[:B], jnp.float32(0.0))
    panel, p_col, e_col, k_part, gram_part = panel_terms(
        strip.T, symmetric[B : 2 * B].T, symmetric, ring, n_row
    )
    r_mat, linv, lead, u_col, v_col = basis(
        n_row, gram_part, k_part, panel[B : 2 * B], p_col, e_col
    )
    u_rows, x, x1, y = product_terms(u_col, v_col, lead, linv, panel, ring, n_row)
    return update(symmetric, panel, u_rows, x1, y, x, r_mat, order)


def solution(mesh):
    n_row = mesh.shape["row"]

    ring = ring_of(mesh)

    def run(symmetric):
        return per_device(ring, n_row, symmetric)

    return jax.shard_map(
        run, mesh=mesh, in_specs=(P("row", "col"),), out_specs=P("row", "col"), check_vma=False
    )
```

```python
import math

import jax
import jax.numpy as jnp
from jax import lax
from jax.experimental import pallas as pl
from jax.experimental.pallas import tpu as pltpu
from jax.sharding import PartitionSpec as P

B = 256
NB = 64
TILE = 768
SUB = 8
MESH = pl.DeviceIdType.MESH
HIGH = lax.Precision.HIGH
HIGHEST = lax.Precision.HIGHEST
VMEM = pl.BlockSpec(memory_space=pltpu.VMEM)


def contract(left_op, right_op, left_dim, right_dim, precision=HIGHEST):
    return lax.dot_general(
        left_op,
        right_op,
        (((left_dim,), (right_dim,)), ((), ())),
        precision=precision,
        preferred_element_type=jnp.float32,
    )


def eye(n):
    rows = lax.broadcasted_iota(jnp.int32, (n, n), 0)
    cols = lax.broadcasted_iota(jnp.int32, (n, n), 1)
    return (rows == cols).astype(jnp.float32)


def eliminate_some(whole, columns, full):
    parts = [whole[8 * g : 8 * g + 8] for g in range(NB // 8)]
    sub = lax.broadcasted_iota(jnp.int32, (8, 2 * NB), 0)
    whole_tile = (8, 2 * NB)
    for j in columns:
        home, at = j // 8, j % 8
        top = jnp.broadcast_to(parts[home][at : at + 1, :], whole_tile)
        low = jnp.broadcast_to(parts[home][at + 1 : at + 2, :], whole_tile)
        top_0 = jnp.broadcast_to(top[:, j : j + 1], whole_tile)
        top_1 = jnp.broadcast_to(top[:, j + 1 : j + 2], whole_tile)
        low_0 = jnp.broadcast_to(low[:, j : j + 1], whole_tile)
        low_1 = jnp.broadcast_to(low[:, j + 1 : j + 2], whole_tile)
        over = 1.0 / top_0
        ratio = low_0 * over
        second = low - ratio * top
        row_1 = second * (1.0 / (low_1 - ratio * top_1))
        row_0 = top * over - (top_1 * over) * row_1
        for g in range(0 if full else home, NB // 8):
            moved = parts[g] - parts[g][:, j : j + 1] * row_0 - parts[g][:, j + 1 : j + 2] * row_1
            if g == home:
                if full:
                    moved = jnp.where(sub == at, row_0, jnp.where(sub == at + 1, row_1, moved))
                else:
                    moved = jnp.where(sub > at + 1, moved, jnp.where(sub == at + 1, second, parts[g]))
            parts[g] = moved
    return jnp.concatenate(parts, axis=0)


def factor_into(gram, r_ref, linv_ref, work):
    work[:, :B] = gram
    work[:, B:] = eye(B)
    for o in range(0, B, NB):
        whole = jnp.concatenate([work[o : o + NB, o : o + NB], eye(NB)], axis=1)
        done = eliminate_some(whole, range(0, NB, 2), False)
        diag = jnp.sum(done[:, :NB] * eye(NB), axis=1, keepdims=True)
        scaled = done[:, NB:] * lax.rsqrt(diag)
        strip = contract(scaled, work[o : o + NB, :], 1, 0)
        rows = o + lax.broadcasted_iota(jnp.int32, (NB, B), 0)
        cols = lax.broadcasted_iota(jnp.int32, (NB, B), 1)
        r_ref[o : o + NB, :] = jnp.where(cols >= rows, strip[:, :B], 0.0)
        linv_ref[o : o + NB, :] = strip[:, B:]
        if o + NB < B:
            below = contract(strip[:, :B], strip, 0, 0)
            work[o + NB :, :] = work[o + NB :, :] - below[o + NB :, :]


def update_kernel(scale, a_ref, p_ref, u_ref, x1_ref, y_ref, x_ref, r_ref, o_ref, right):
    step = pl.program_id(0)
    row_at = lax.axis_index("row")
    col_at = lax.axis_index("col")
    cols_dev = a_ref.shape[1]

    @pl.when(step == 0)
    def _():
        for at, ref in ((0, x1_ref), (3, y_ref)):
            high, low = split(ref[...])
            right[at * B : (at + 1) * B, :] = high
            right[(at + 1) * B : (at + 2) * B, :] = high
            right[(at + 2) * B : (at + 3) * B, :] = low

    p_high, p_low = split(p_ref[...])
    u_high, u_low = split(u_ref[...])
    left = jnp.concatenate([p_high, p_low, p_high, u_high, u_low, u_high], axis=1)
    o_ref[...] = a_ref[...] - jnp.dot(left, right[...], preferred_element_type=jnp.float32)

    first = jnp.logical_and(step == 0, row_at == 0)

    @pl.when(first)
    def _():
        o_ref[B : 2 * B, :] = o_ref[B : 2 * B, :] + x_ref[...]
        global_cols = col_at * cols_dev + lax.broadcasted_iota(jnp.int32, (B, cols_dev), 1)
        band = lax.broadcasted_iota(jnp.int32, (B, cols_dev), 0)
        onehot = (global_cols - B == band).astype(jnp.float32)
        mirror = contract(r_ref[...] * scale, onehot, 0, 0)
        o_ref[:B, :] = jnp.where(global_cols >= B, mirror, o_ref[:B, :])

    @pl.when(jnp.logical_and(first, col_at == 0))
    def _():
        o_ref[B : 2 * B, :B] = r_ref[...] * scale

    @pl.when(jnp.logical_and(jnp.logical_not(first), col_at == 0))
    def _():
        o_ref[:, :B] = jnp.zeros((TILE, B), jnp.float32)


def update(current, panel, u_rows, x1, y, x, r_mat, order):
    rows_dev, cols_dev = current.shape
    tall = pl.BlockSpec((TILE, B), lambda i: (i, 0))
    flat = pl.BlockSpec((B, cols_dev), lambda i: (0, 0))
    wide = pl.BlockSpec((TILE, cols_dev), lambda i: (i, 0))
    scale = 1.0 / math.sqrt(order)

    def kernel(*refs):
        update_kernel(scale, *refs)

    return pl.pallas_call(
        kernel,
        grid=(rows_dev // TILE,),
        out_shape=jax.ShapeDtypeStruct((rows_dev, cols_dev), jnp.float32),
        in_specs=[wide, tall, tall, flat, flat, flat, pl.BlockSpec((B, B), lambda i: (0, 0))],
        out_specs=wide,
        scratch_shapes=[pltpu.VMEM((6 * B, cols_dev), jnp.bfloat16)],
        compiler_params=pltpu.CompilerParams(vmem_limit_bytes=48 * 1024 * 1024),
    )(current, panel, u_rows, x1, y, x, r_mat)


def ring_of(mesh):
    coords = [tuple(d.coords) for d in mesh.devices[0][::2]]
    moving = [i for i in range(3) if len({c[i] for c in coords}) > 1]
    index = {c: i for i, c in enumerate(coords)}
    long_axis, short_axis = moving[0], moving[-1]
    tall = sorted({c[long_axis] for c in coords})
    flat = sorted({c[short_axis] for c in coords})

    def chip(a, b):
        at = list(coords[0])
        at[long_axis], at[short_axis] = tall[a], flat[b]
        return index[tuple(at)]

    order = [chip(a, 0) for a in range(len(tall) - 1, -1, -1)]
    for a in range(len(tall)):
        across = range(1, len(flat)) if a % 2 == 0 else range(len(flat) - 1, 0, -1)
        order += [chip(a, b) for b in across]
    return order


def look_up(table, at):
    found = jnp.int32(table[0])
    for i in range(1, len(table)):
        found = jnp.where(at == i, jnp.int32(table[i]), found)
    return found


def ring_gather(ring, n_row, out_ref, first_ref, sems):
    ring_send, ring_recv, sib_send, sib_recv = sems
    row_at, col_at = lax.axis_index("row"), lax.axis_index("col")
    n = len(ring)
    rows = first_ref.shape[0]
    cut = rows // SUB
    chip, core = col_at // 2, lax.rem(col_at, 2)
    per_plane = n // n_row
    place = look_up([ring.index(i) for i in range(n)], chip)
    way = 1 - 2 * core
    next_col = 2 * look_up(ring, lax.rem(place + way + n, n)) + core
    prev_col = 2 * look_up(ring, lax.rem(place - way + n, n)) + core
    sib_col = 2 * chip + 1 - core

    barrier = pltpu.get_barrier_semaphore()
    for col in (next_col, prev_col, sib_col):
        pl.semaphore_signal(barrier, inc=1, device_id=(row_at, col), device_id_type=MESH)
    for other in peers(n_row, row_at):
        pl.semaphore_signal(barrier, inc=1, device_id=(other, col_at), device_id_type=MESH)
    pl.semaphore_wait(barrier, 3 + n_row - 1)

    def start_of(source, of_core):
        return pl.multiple_of((source * 2 + of_core) * rows, 8)

    def window(source, of_core, sub):
        return out_ref.at[pl.ds(pl.multiple_of(start_of(source, of_core) + sub * cut, 8), cut)]

    def ring_copy(source, sub, src):
        return pltpu.make_async_remote_copy(
            src_ref=src,
            dst_ref=window(source, core, sub),
            send_sem=ring_send.at[source, sub],
            recv_sem=ring_recv.at[source, sub],
            device_id=(row_at, next_col),
            device_id_type=MESH,
        )

    def sib_copy(source, of_core, sub, src):
        return pltpu.make_async_remote_copy(
            src_ref=src,
            dst_ref=window(source, of_core, sub),
            send_sem=sib_send.at[source, sub],
            recv_sem=sib_recv.at[source, sub],
            device_id=(row_at, sib_col),
            device_id_type=MESH,
        )

    def found(step, turn):
        at = look_up(ring, lax.rem(place - turn * step + n, n))
        source = at - row_at * per_plane
        valid = jnp.logical_and(source >= 0, source < per_plane)
        return valid, jnp.clip(source, 0, per_plane - 1)

    has_home, home = found(0, way)

    def begin(sub, src_ref):
        src = src_ref.at[pl.ds(sub * cut, cut)]
        ring_copy(home, sub, src).start()
        sib_copy(home, core, sub, src).start()

    def keep(src_ref):
        out_ref[pl.ds(start_of(home, core), rows), :] = src_ref[...]

    def forward(step, sub):
        valid, source = found(step, way)

        @pl.when(valid)
        def _():
            src = window(source, core, sub)
            ring_copy(source, sub, src).wait_recv()

            @pl.when(step < n - 1)
            def _():
                ring_copy(source, sub, src).start()

            sib_copy(source, core, sub, src).start()

    def from_sibling(source):
        for sub in range(SUB):
            sib_copy(source, 1 - core, sub, window(source, core, sub)).wait_recv()

    def finish():
        def sent(step, carry):
            valid, source = found(step, way)

            @pl.when(valid)
            def _():
                for sub in range(SUB):
                    src = window(source, core, sub)

                    @pl.when(step < n - 1)
                    def _():
                        ring_copy(source, sub, src).wait_send()

                    sib_copy(source, core, sub, src).wait_send()

            return carry

        lax.fori_loop(0, n, sent, 0)

    return dict(
        n=n, way=way, core=core, has_home=has_home, start_of=start_of, found=found, begin=begin, keep=keep,
        forward=forward, from_sibling=from_sibling, finish=finish,
    )


def split(value):
    high = value.astype(jnp.bfloat16)
    low = (value - high.astype(jnp.float32)).astype(jnp.bfloat16)
    return high, low


def product(left_op, right_op):
    left_high, left_low = split(left_op)
    right_high, right_low = split(right_op)
    left = jnp.concatenate([left_high, left_low, left_high], axis=0)
    right = jnp.concatenate([right_high, right_high, right_low], axis=0)
    return lax.dot_general(
        left, right, (((0,), (0,)), ((), ())), preferred_element_type=jnp.float32
    )


def panel_kernel(
    ring, n_row, first_ref, extra_ref, a_ref, out_ref, chunk_ref, beside_ref, k_ref, gram_ref, lead_ref,
    held, a_sem, ring_send, ring_recv, sib_send, sib_recv, hop_send, hop_recv, beside_send, beside_recv,
):
    row_at, col_at = lax.axis_index("row"), lax.axis_index("col")
    rows = first_ref.shape[0]
    cut = rows // SUB
    load = pltpu.make_async_copy(a_ref, held, a_sem)
    load.start()
    g = ring_gather(ring, n_row, out_ref, first_ref, (ring_send, ring_recv, sib_send, sib_recv))
    has_home = g["has_home"]

    def hop_copy(other, sub):
        return pltpu.make_async_remote_copy(
            src_ref=first_ref.at[pl.ds(sub * cut, cut)],
            dst_ref=chunk_ref.at[pl.ds(sub * cut, cut)],
            send_sem=hop_send.at[other - 1, sub],
            recv_sem=hop_recv.at[sub],
            device_id=(other, col_at),
            device_id_type=MESH,
        )

    def beside_copy(other):
        return pltpu.make_async_remote_copy(
            src_ref=extra_ref,
            dst_ref=beside_ref,
            send_sem=beside_send.at[other - 1],
            recv_sem=beside_recv,
            device_id=(other, col_at),
            device_id_type=MESH,
        )

    @pl.when(row_at == 0)
    def _():
        for sub in range(SUB):
            @pl.when(has_home)
            def _():
                g["begin"](sub, first_ref)

            for other in range(1, n_row):
                hop_copy(other, sub).start()
        for other in range(1, n_row):
            beside_copy(other).start()
        chunk_ref[...] = first_ref[...]
        beside_ref[...] = extra_ref[...]

        @pl.when(has_home)
        def _():
            g["keep"](first_ref)

    @pl.when(jnp.logical_and(row_at > 0, has_home))
    def _():
        for sub in range(SUB):
            hop_copy(1, sub).wait_recv()
            g["begin"](sub, chunk_ref)
        g["keep"](chunk_ref)

    k_ref[...] = jnp.zeros_like(k_ref)
    gram_ref[...] = jnp.zeros_like(gram_ref)
    load.wait()

    part = rows // 2

    def absorb(source, of_core, half):
        start = g["start_of"](source, of_core) + half * part
        at = pl.ds(pl.multiple_of(start, 8), part)
        panel = out_ref[at, :]
        k_ref[...] += product(panel, held[at, :])
        gram_ref[...] += contract(panel, panel, 0, 0)

    def own_part(step, half):
        valid, source = g["found"](step, g["way"])

        @pl.when(valid)
        def _():
            absorb(source, g["core"], half)

    def sibling_part(step, half):
        valid, source = g["found"](step, -g["way"])

        @pl.when(valid)
        def _():
            if half == 0:
                g["from_sibling"](source)
            absorb(source, 1 - g["core"], half)

    works = [(own_part, 0), (own_part, 1), (sibling_part, 0), (sibling_part, 1)]

    def step_on(step, carry):
        for at, (work, half) in enumerate(works):
            for sub in range(at * SUB // 4, (at + 1) * SUB // 4):
                g["forward"](step, sub)
            work(step - 1, half)
        return carry

    lax.fori_loop(1, g["n"], step_on, 0)
    for work, half in works:
        work(g["n"] - 1, half)
    lead_ref[...] = out_ref[B : 2 * B, :]
    g["finish"]()

    @pl.when(row_at == 0)
    def _():
        for other in range(1, n_row):
            for sub in range(SUB):
                hop_copy(other, sub).wait_send()
            beside_copy(other).wait_send()

    @pl.when(row_at > 0)
    def _():
        beside_copy(1).wait_recv()

    @pl.when(jnp.logical_and(row_at > 0, jnp.logical_not(has_home)))
    def _():
        for sub in range(SUB):
            hop_copy(1, sub).wait_recv()


def panel_terms(first, extra, symmetric, ring, n_row):
    per_plane = len(ring) // n_row
    dma = pltpu.SemaphoreType.DMA
    rows = first.shape[0]

    def kernel(*refs):
        panel_kernel(ring, n_row, *refs)

    def shape(*dims):
        return jax.ShapeDtypeStruct(dims, jnp.float32)

    return pl.pallas_call(
        kernel,
        out_shape=(
            shape(symmetric.shape[0], B), shape(rows, B), shape(rows, B), shape(B, rows), shape(B, B),
            shape(B, B),
        ),
        in_specs=[VMEM, VMEM, pl.BlockSpec(memory_space=pl.ANY)],
        out_specs=(VMEM,) * 6,
        scratch_shapes=[pltpu.VMEM(symmetric.shape, jnp.float32), dma]
        + [dma((per_plane, SUB))] * 4
        + [dma((n_row - 1, SUB)), dma((SUB,)), dma((n_row - 1,)), dma],
        compiler_params=pltpu.CompilerParams(
            collective_id=1, has_side_effects=True, vmem_limit_bytes=56 * 1024 * 1024
        ),
    )(first, extra, symmetric)


def inverse_tasks(lead_ref, linv_ref, t_ref, work, block):
    tasks = []

    def begin():
        work[:, :B] = eye(B) - contract(lead_ref[...], linv_ref[...], 1, 1)
        work[:, B:] = eye(B)

    tasks.append(begin)
    for o in range(0, B, NB):
        def load(o=o):
            block[...] = jnp.concatenate([work[o : o + NB, o : o + NB], eye(NB)], axis=1)

        tasks.append(load)
        for j in range(0, NB, 4):
            def some(j=j):
                block[...] = eliminate_some(block[...], range(j, j + 4, 2), True)

            tasks.append(some)

        def spread(o=o):
            strip = contract(block[:, NB:], work[o : o + NB, :], 1, 0)
            change = contract(work[:, o : o + NB], strip, 1, 0)
            work[...] = work[...] - change
            work[o : o + NB, :] = strip

        tasks.append(spread)

    def end():
        t_ref[...] = work[:, B:]

    tasks.append(end)
    return tasks


def product_kernel(
    ring, n_row, u_ref, v_ref, lead_ref, linv_ref, panel_ref, out_ref, x_ref, x1_ref, y_ref,
    t_ref, work, block, z_ref, z_in, ring_send, ring_recv, sib_send, sib_recv, z_send, z_recv,
):
    row_at, col_at = lax.axis_index("row"), lax.axis_index("col")
    rows = u_ref.shape[0]
    g = ring_gather(ring, n_row, out_ref, u_ref, (ring_send, ring_recv, sib_send, sib_recv))
    has_home, n = g["has_home"], g["n"]

    @pl.when(has_home)
    def _():
        for sub in range(SUB):
            g["begin"](sub, u_ref)
        g["keep"](u_ref)

    tasks = inverse_tasks(lead_ref, linv_ref, t_ref, work, block)
    slots = (n - 1) * SUB
    done = 0
    for slot in range(slots):
        g["forward"](1 + slot // SUB, slot % SUB)
        until = (slot + 1) * len(tasks) // slots
        for task in tasks[done:until]:
            task()
        done = until
    t_mat = t_ref[...]
    y_ref[...] = contract(t_mat, v_ref[...], 0, 1)
    x_ref[...] = contract(t_mat, u_ref[...], 1, 1)
    z_ref[...] = jnp.zeros_like(z_ref)

    def absorb(source, carry):
        g["from_sibling"](source)
        at = pl.ds(pl.multiple_of(source * 2 * rows, 8), 2 * rows)
        z_ref[...] += product(panel_ref[at, :], out_ref[at, :])
        return carry

    lax.fori_loop(0, n // n_row, absorb, 0)
    own = jnp.where(row_at == 0, out_ref[B : 2 * B, :], 0.0)
    z_ref[...] = contract(linv_ref[...], z_ref[...], 1, 0) - own
    copies = exchange(n_row, row_at, col_at, z_ref, z_in, z_send, z_recv)
    g["finish"]()
    core_sum = total(n_row, z_ref, z_in, copies)
    middle = contract(contract(t_mat, core_sum, 1, 0), t_mat, 1, 1)
    x = x_ref[...] - contract(middle, v_ref[...], 1, 1)
    x_ref[...] = x
    x1_ref[...] = contract(linv_ref[...], x, 0, 0)
    for copy in copies:
        copy.wait_send()


def product_terms(u_col, v_col, lead, linv, panel, ring, n_row):
    per_plane = len(ring) // n_row
    dma = pltpu.SemaphoreType.DMA
    flat = jax.ShapeDtypeStruct(u_col.shape[::-1], jnp.float32)

    def kernel(*refs):
        product_kernel(ring, n_row, *refs)

    def scratch(*dims):
        return pltpu.VMEM(dims, jnp.float32)

    return pl.pallas_call(
        kernel,
        out_shape=(jax.ShapeDtypeStruct(panel.shape, jnp.float32), flat, flat, flat),
        in_specs=[VMEM] * 5,
        out_specs=(VMEM,) * 4,
        scratch_shapes=[
            scratch(B, B), scratch(B, 2 * B), scratch(NB, 2 * NB), scratch(B, B), scratch(n_row - 1, B, B)
        ]
        + [dma((per_plane, SUB))] * 4
        + [dma((n_row - 1,))] * 2,
        compiler_params=pltpu.CompilerParams(
            collective_id=3, has_side_effects=True, vmem_limit_bytes=56 * 1024 * 1024
        ),
    )(u_col, v_col, lead, linv, panel)


def peers(n_row, row_at):
    return [lax.rem(row_at + d, n_row) for d in range(1, n_row)]


def greet(n_row, row_at, col_at):
    barrier = pltpu.get_barrier_semaphore()
    for other in peers(n_row, row_at):
        pl.semaphore_signal(barrier, inc=1, device_id=(other, col_at), device_id_type=MESH)
    pl.semaphore_wait(barrier, n_row - 1)


def exchange(n_row, row_at, col_at, src, landing, send, recv):
    copies = []
    for at, other in enumerate(peers(n_row, row_at)):
        copy = pltpu.make_async_remote_copy(
            src_ref=src,
            dst_ref=landing.at[at],
            send_sem=send.at[at],
            recv_sem=recv.at[at],
            device_id=(other, col_at),
            device_id_type=MESH,
        )
        copy.start()
        copies.append(copy)
    return copies


def total(n_row, src, landing, copies):
    for copy in copies:
        copy.wait_recv()
    found = src[...]
    for at in range(n_row - 1):
        found = found + landing[at]
    return found


def basis_kernel(
    n_row, gram_ref, k_ref, lead_ref, p_ref, e_ref, r_ref, linv_ref, lead_out, u_ref, v_ref,
    work, gram_in, k_in, gram_send, gram_recv, k_send, k_recv, lead_send, lead_recv,
):
    row_at, col_at = lax.axis_index("row"), lax.axis_index("col")
    greet(n_row, row_at, col_at)
    gram_copies = exchange(n_row, row_at, col_at, gram_ref, gram_in, gram_send, gram_recv)

    def lead_copy(other):
        return pltpu.make_async_remote_copy(
            src_ref=lead_ref,
            dst_ref=lead_out,
            send_sem=lead_send.at[other - 1],
            recv_sem=lead_recv,
            device_id=(other, col_at),
            device_id_type=MESH,
        )

    k_copies = exchange(n_row, row_at, col_at, k_ref, k_in, k_send, k_recv)

    @pl.when(row_at == 0)
    def _():
        for other in range(1, n_row):
            lead_copy(other).start()
        lead_out[...] = lead_ref[...]

    gram = total(n_row, gram_ref, gram_in, gram_copies)
    factor_into(gram, r_ref, linv_ref, work)
    linv = linv_ref[...]
    cols_dev = p_ref.shape[0]
    global_cols = col_at * cols_dev + lax.broadcasted_iota(jnp.int32, (cols_dev, B), 0)
    band = lax.broadcasted_iota(jnp.int32, (cols_dev, B), 1)
    col_unit = (global_cols - B == band).astype(jnp.float32)
    v_ref[...] = contract(p_ref[...], linv, 1, 1) - col_unit
    q_col = total(n_row, k_ref, k_in, k_copies)
    u_ref[...] = contract(q_col, linv, 0, 1) - e_ref[...]
    for copy in gram_copies + k_copies:
        copy.wait_send()

    @pl.when(row_at == 0)
    def _():
        for other in range(1, n_row):
            lead_copy(other).wait_send()

    @pl.when(row_at > 0)
    def _():
        lead_copy(1).wait_recv()


def basis(n_row, gram, k, lead, p_col, e_col):
    dma = pltpu.SemaphoreType.DMA
    small = jax.ShapeDtypeStruct((B, B), jnp.float32)
    part = jax.ShapeDtypeStruct(p_col.shape, jnp.float32)
    others = dma((n_row - 1,))

    def kernel(*refs):
        basis_kernel(n_row, *refs)

    return pl.pallas_call(
        kernel,
        out_shape=(small, small, small, part, part),
        in_specs=[VMEM] * 5,
        out_specs=(VMEM,) * 5,
        scratch_shapes=[
            pltpu.VMEM((B, 2 * B), jnp.float32),
            pltpu.VMEM((n_row - 1, B, B), jnp.float32),
            pltpu.VMEM((n_row - 1,) + k.shape, jnp.float32),
            others, others, others, others, others, dma,
        ],
        compiler_params=pltpu.CompilerParams(
            collective_id=2, has_side_effects=True, vmem_limit_bytes=48 * 1024 * 1024
        ),
    )(gram, k, lead, p_col, e_col)


def per_device(ring, n_row, symmetric):
    cols_dev = symmetric.shape[1]
    order = symmetric.shape[0] * n_row
    global_cols = lax.axis_index("col") * cols_dev + jnp.arange(cols_dev, dtype=jnp.int32)

    strip = jnp.where((global_cols >= B)[None, :], symmetric[:B], jnp.float32(0.0))
    panel, p_col, e_col, k_part, gram_part, lead_part = panel_terms(
        strip.T, symmetric[B : 2 * B].T, symmetric, ring, n_row
    )
    r_mat, linv, lead, u_col, v_col = basis(
        n_row, gram_part, k_part, lead_part, p_col, e_col
    )
    u_rows, x, x1, y = product_terms(u_col, v_col, lead, linv, panel, ring, n_row)
    return update(symmetric, panel, u_rows, x1, y, x, r_mat, order)


def solution(mesh):
    n_row = mesh.shape["row"]

    ring = ring_of(mesh)

    def run(symmetric):
        return per_device(ring, n_row, symmetric)

    return jax.shard_map(
        run, mesh=mesh, in_specs=(P("row", "col"),), out_specs=P("row", "col"), check_vma=False
    )
```
